32 devices in a mesh: groups: 2 (over x), slab: 16 (over z, y, core).
Axes of the slice: x: 2, y: 2, z: 4, core: 2. Of those that a mesh axis runs over, the one named last changes fastest.
Arguments:
- queries: bfloat16 [32, 32, 128], P(('groups', 'slab')), parts along dimension 0, may hold values from -6 to 6
- passages: bfloat16 [2048, 128, 128], P(('groups', 'slab')), parts along dimension 0, may hold values from -0.5 to 0.5
- lengths: int32 [2048], P(('groups', 'slab')), parts along dimension 0, may hold values from 1 to 128
- shortlist: int32 [32, 96], P(('groups', 'slab')), parts along dimension 0, may hold values from 0 to 1023, as said below
Outputs:
- coarse: float32 [2048, 16], P(('groups', 'slab')), parts along dimension 0
- exact: float32 [32, 96], P(('groups', 'slab')), parts along dimension 0
The draws below stay inside these ranges and needn't reach their ends.
There are 2 independent parts, one for each index of `groups`. The reference program is written for one: setup_inputs(seed, part) draws one part's arguments, and reference() takes and returns one part's arrays. A program takes and returns all parts, laid end to end along the dimension named above; each array names one. Nothing has to cross between parts.
Inputs may be any that keep to these rules, and one draw needn't show every extreme that they name: `shortlist`: passage id p lies on slab p // 64. The ids of one query are distinct; at most 16 of them lie on any one slab, and in every draw one slab holds exactly 16 ids of every query.
All inputs are finite; a program needn't handle non-finite values.
Results may differ from the reference program's by a relative error of at most 0.00037.
Values may be sent and summed in bfloat16 or wider, within the bound.
No kernel may reach another device: no remote copies, remote signals or barrier semaphores. Data moves between devices by JAX's collectives and lax.ppermute only.
A program may use at most 128 MiB of HBM per device.

```python
import jax
import jax.numpy as jnp
from jax import lax

DIM = 128
PREFIX = 64
Q_TOK = 32
P_TOK = 128
P_DEV = 64
SHORT = 96
QUERIES = 16
PASSAGES = 1024
CAP = 16


def draw_shortlist(key, part):
    key = jax.random.fold_in(key, 11)
    owners = PASSAGES // P_DEV
    key_heavy, key_hot, key_base, key_noise = jax.random.split(key, 4)
    heavy = jax.random.randint(key_heavy, (), 0, owners)
    hot = jnp.where(jax.random.randint(key_hot, (owners,), 0, 8) == 0, 8, 1)
    slot_owner = jnp.repeat(jnp.arange(owners, dtype=jnp.int32), CAP)
    slot_copy = jnp.tile(jnp.arange(CAP, dtype=jnp.int32), owners)
    base = jax.random.randint(key_base, (QUERIES, owners), 0, P_DEV)
    noise = jax.random.randint(key_noise, (QUERIES, owners * CAP), 0, 4096)
    order = jnp.arange(owners * CAP, dtype=jnp.int32)
    score = noise * hot[slot_owner][None, :] * (owners * CAP) + order[None, :]
    score = jnp.where(slot_owner[None, :] == heavy, 2 ** 30 + order[None, :], score)
    picked = lax.top_k(score, SHORT)[1]
    owner = slot_owner[picked]
    copy_index = slot_copy[picked]
    local = (jnp.take_along_axis(base, owner, axis=1) + copy_index) % P_DEV
    return (owner * P_DEV + local).astype(jnp.int32)


def touch_ends(entries, key, least, top_value):
    dims = entries.shape
    place = [jax.random.randint(jax.random.fold_in(key, axis), (), 0, dims[axis]) for axis in range(len(dims))]
    entries = entries.at[tuple(place)].set(least)
    longest = dims.index(max(dims))
    place[longest] = (place[longest] + 1) % dims[longest]
    return entries.at[tuple(place)].set(top_value)


def levels(rng, dims, pieces, low, largest):
    level, own = 1.0, jax.random.fold_in(rng, 6)
    for axis_at, parts in pieces:
        steps = jnp.exp(jax.random.uniform(jax.random.fold_in(own, axis_at), (parts,), jnp.float32, low / len(pieces), largest / len(pieces)))
        level = level * jnp.repeat(steps, dims[axis_at] // parts).reshape([-1 if axis == axis_at else 1 for axis in range(len(dims))])
    return level


def scatter_about(rng, shape, deviation, bound, cuts=(), held_as=jnp.bfloat16):
    factor_of = levels(rng, shape, cuts, -0.22, 0.18) if cuts else 1.0
    drawn = jax.random.normal(rng, shape, jnp.float32) * deviation * factor_of
    return jnp.minimum(jnp.maximum(drawn, -bound), bound).astype(held_as)


def setup_inputs(seed: int = 0, part: int = 0) -> dict:
    splits = jax.random.split(jax.random.key(seed), 5)
    part_keys = jax.random.split(jax.random.fold_in(splits[4], part), 5)
    queries = scatter_about(part_keys[0], (QUERIES, Q_TOK, DIM), 1.0, 6.0, ((0, 16),))
    passages = scatter_about(part_keys[1], (PASSAGES, P_TOK, DIM), DIM ** -0.5, 0.5, ((0, 16),))
    lengths = touch_ends(jax.random.randint(part_keys[2], (PASSAGES,), 1, P_TOK + 1), jax.random.fold_in(part_keys[2], 1), 1, P_TOK).astype(jnp.int32)
    shortlist = draw_shortlist(jax.random.fold_in(jax.random.fold_in(splits[4], part), 71), part)
    return dict(queries=queries, passages=passages, lengths=lengths, shortlist=shortlist)


def unit_prefix(vectors):
    head = vectors[..., :PREFIX].astype(jnp.float32)
    total = lax.optimization_barrier(jnp.sum(head * head, axis=-1, keepdims=True))
    return (head * lax.rsqrt(total + 1e-06)).astype(jnp.bfloat16)

def reference(queries, passages, lengths, shortlist):
    query_prefix = unit_prefix(queries).astype(jnp.float32).reshape(QUERIES * Q_TOK, PREFIX)
    passage_prefix = unit_prefix(passages)
    group = 64 if PASSAGES % 64 == 0 else 8
    blocks = passage_prefix.reshape(PASSAGES // group, group * P_TOK, PREFIX)
    block_lens = lengths.reshape(PASSAGES // group, group)
    slots = jnp.arange(P_TOK, dtype=jnp.int32)

    def one_block(item):
        block, lens = item
        scores = jnp.dot(query_prefix, block.astype(jnp.float32).T)
        scores = scores.reshape(QUERIES, Q_TOK, group, P_TOK)
        scores = jnp.where(slots[None, None, None, :] < lens[None, None, :, None], scores, -1e+30)
        return lax.optimization_barrier(jnp.mean(lax.optimization_barrier(jnp.max(scores, axis=-1)), axis=1))
    coarse = lax.map(one_block, (blocks, block_lens))
    coarse = jnp.transpose(coarse, (0, 2, 1)).reshape(PASSAGES, QUERIES)

    def one_query(item):
        query, ids = item
        chosen = passages[ids].astype(jnp.float32)
        lens = lengths[ids]
        scores = jnp.einsum('td,jud->jtu', query.astype(jnp.float32), chosen)
        scores = jnp.where(slots[None, None, :] < lens[:, None, None], scores, -1e+30)
        return lax.optimization_barrier(jnp.mean(lax.optimization_barrier(jnp.max(scores, axis=-1)), axis=-1))
    exact = lax.map(one_query, (queries, shortlist))
    return (coarse, exact)
```

```python
import functools

import jax
import jax.numpy as jnp
from jax import lax
from jax.experimental import pallas as pl
from jax.experimental.pallas import tpu as pltpu
from jax.sharding import PartitionSpec as P

PREFIX = 64
EPS = 1e-06
VMEM = pl.BlockSpec(memory_space=pltpu.VMEM)
SMEM = pl.BlockSpec(memory_space=pltpu.SMEM)


def params():
    return pltpu.CompilerParams(vmem_limit_bytes=24 << 20)


def unit_prefix(rows):
    head = rows[:, :PREFIX]
    total = jnp.sum(head * head, axis=-1, keepdims=True)
    return (head * lax.rsqrt(total + EPS)).astype(jnp.bfloat16)


def prepare_kernel(count, width, lens_ref, passages_ref, full_ref, prefix_ref):
    row = lax.broadcasted_iota(jnp.int32, (width, passages_ref.shape[2]), 0)
    for p in range(count):
        tokens = passages_ref[p].astype(jnp.float32)
        tokens = jnp.where(row < lens_ref[p], tokens, tokens[0:1])
        at = pl.ds(p * width, width)
        full_ref[at, :] = tokens.astype(jnp.bfloat16)
        prefix_ref[at, :] = unit_prefix(tokens)


def prepare(lengths, passages):
    count, width, dim = passages.shape
    return pl.pallas_call(
        functools.partial(prepare_kernel, count, width),
        out_shape=(
            jax.ShapeDtypeStruct((count * width, dim), jnp.bfloat16),
            jax.ShapeDtypeStruct((count * width, PREFIX), jnp.bfloat16),
        ),
        in_specs=[SMEM, VMEM],
        out_specs=(VMEM, VMEM),
        compiler_params=params(),
        cost_estimate=pl.CostEstimate(flops=count * width * dim * 8, bytes_accessed=9 << 20, transcendentals=0),
    )(lengths, passages)


def maxima(tokens_ref, queries, best_ref, count, width):
    step = 256
    rows = queries.shape[0]
    for at in range(0, rows, step):
        block = queries[at : at + step, :]
        for p in range(0, count, 2):
            scores = lax.dot_general(
                tokens_ref[p * width : (p + 2) * width, :],
                block,
                (((1,), (1,)), ((), ())),
                preferred_element_type=jnp.float32,
            )
            best_ref[p : p + 2, at : at + step] = jnp.max(scores.reshape(2, width, step), axis=1)


def averaging(me, queries, qtok):
    shape = (queries, queries * qtok)
    place = lax.broadcasted_iota(jnp.int32, shape, 1) // qtok
    whose = lax.broadcasted_iota(jnp.int32, shape, 0)
    return jnp.where((place ^ me) == whose, 1.0 / qtok, 0.0).astype(jnp.float32)


def average(me, best, owners):
    mean = averaging(me, owners, best.shape[1] // owners)
    return lax.dot_general(
        mean, best, (((1,), (1,)), ((), ())), preferred_element_type=jnp.float32, precision=lax.Precision.HIGHEST
    )


def exact_kernel(count, width, owners, me_ref, tokens_ref, queries_ref, out_ref, best_ref):
    maxima(tokens_ref, queries_ref[...], best_ref, count, width)
    out_ref[...] = average(me_ref[0], best_ref[...], owners)


def coarse_kernel(count, width, owners, me_ref, tokens_ref, queries_ref, out_ref, best_ref):
    maxima(tokens_ref, unit_prefix(queries_ref[...].astype(jnp.float32)), best_ref, count, width)
    out_ref[...] = average(me_ref[0], best_ref[...], owners)


def score(kernel, me, tokens, queries, owners, count):
    width = tokens.shape[0] // count
    return pl.pallas_call(
        functools.partial(kernel, count, width, owners),
        out_shape=jax.ShapeDtypeStruct((owners, count), jnp.float32),
        in_specs=[SMEM, VMEM, VMEM],
        out_specs=VMEM,
        scratch_shapes=[pltpu.VMEM((count, queries.shape[0]), jnp.float32)],
        compiler_params=params(),
        cost_estimate=pl.CostEstimate(
            flops=4 * tokens.shape[0] * queries.shape[0] * 128, bytes_accessed=4 << 20, transcendentals=0
        ),
    )(me, tokens, queries)


def pick_kernel(ids_ref, returned_ref, out_ref):
    owners, count = returned_ref.shape
    ids = ids_ref[...]
    owner, local = ids // count, ids % count
    short = ids.shape[1]
    hot = lax.broadcasted_iota(jnp.int32, (count, short), 0) == local
    column = lax.dot_general(
        returned_ref[...],
        hot.astype(jnp.float32),
        (((1,), (0,)), ((), ())),
        preferred_element_type=jnp.float32,
        precision=lax.Precision.HIGHEST,
    )
    mine = lax.broadcasted_iota(jnp.int32, (owners, short), 0) == owner
    out_ref[...] = jnp.sum(jnp.where(mine, column, 0.0), axis=0, keepdims=True)


def per_device(queries, passages, lengths, shortlist):
    owners = lax.axis_size("slab")
    count = passages.shape[0]
    me = lax.axis_index("slab").astype(jnp.int32).reshape(1)
    full, prefix = prepare(lengths, passages)
    held = queries
    bit = 1
    while bit < owners:
        other = lax.ppermute(held, "slab", [(i, i ^ bit) for i in range(owners)])
        held = jnp.concatenate([held, other], axis=0)
        bit *= 2
    rows = held.reshape(owners * held.shape[1], held.shape[2])
    found = score(exact_kernel, me, full, rows, owners, count)
    returned = lax.all_to_all(found, "slab", split_axis=0, concat_axis=0, tiled=True)
    coarse = score(coarse_kernel, me, prefix, rows, owners, count)
    exact = pl.pallas_call(
        pick_kernel,
        out_shape=jax.ShapeDtypeStruct(shortlist.shape, jnp.float32),
        in_specs=[VMEM, VMEM],
        out_specs=VMEM,
    )(shortlist, returned)
    return (coarse.T, exact)


def solution(mesh):
    return jax.shard_map(
        per_device,
        mesh=mesh,
        in_specs=(
            P(("groups", "slab"), None, None),
            P(("groups", "slab"), None, None),
            P(("groups", "slab")),
            P(("groups", "slab"), None),
        ),
        out_specs=(P(("groups", "slab"), None), P(("groups", "slab"), None)),
        check_vma=False,
    )
```

```python
import functools

import jax
import jax.numpy as jnp
from jax import lax
from jax.experimental import pallas as pl
from jax.experimental.pallas import tpu as pltpu
from jax.sharding import PartitionSpec as P

PREFIX = 64
EPS = 1e-06
CHUNKS = 8
VMEM = pl.BlockSpec(memory_space=pltpu.VMEM)
ANY = pl.BlockSpec(memory_space=pl.ANY)
HBM = pl.BlockSpec(memory_space=pltpu.HBM)


def params(mib=16):
    return pltpu.CompilerParams(vmem_limit_bytes=mib << 20)


def unit_prefix(rows):
    head = rows[:, :PREFIX]
    total = jnp.sum(head * head, axis=-1, keepdims=True)
    return (head * lax.rsqrt(total + EPS)).astype(jnp.bfloat16)


def live_kernel(lens_hbm, passages_hbm, full_ref, lens_ref, passages_ref, sems):
    count, width, dim = passages_ref.shape
    size = count // CHUNKS
    lens_copy = pltpu.make_async_copy(lens_hbm, lens_ref, sems.at[CHUNKS])
    lens_copy.start()
    copies = []
    for c in range(CHUNKS):
        part = pl.ds(c * size, size)
        copies.append(pltpu.make_async_copy(passages_hbm.at[part], passages_ref.at[part], sems.at[c]))
        copies[-1].start()
    lens_copy.wait()
    row = lax.broadcasted_iota(jnp.int32, (width, dim), 0)
    for p in range(count):
        if p % size == 0:
            copies[p // size].wait()
        tokens = passages_ref[p].astype(jnp.float32)
        tokens = jnp.where(row < lens_ref[p], tokens, tokens[0:1])
        full_ref[pl.ds(p * width, width), :] = tokens.astype(jnp.bfloat16)


def live_tokens(lengths, passages):
    count, width, dim = passages.shape
    return pl.pallas_call(
        live_kernel,
        out_shape=jax.ShapeDtypeStruct((count * width, dim), jnp.bfloat16),
        in_specs=[HBM, HBM],
        out_specs=VMEM,
        scratch_shapes=[
            pltpu.SMEM((count,), jnp.int32),
            pltpu.VMEM((count, width, dim), jnp.bfloat16),
            pltpu.SemaphoreType.DMA((CHUNKS + 1,)),
        ],
        compiler_params=params(50),
        cost_estimate=pl.CostEstimate(flops=count * width * dim * 8, bytes_accessed=6 << 20, transcendentals=0),
    )(lengths, passages)


def prefix_kernel(full_ref, prefix_ref):
    width = 128
    for at in range(0, full_ref.shape[0], width):
        prefix_ref[at : at + width, :] = unit_prefix(full_ref[at : at + width, :].astype(jnp.float32))


def prefixes(full):
    return pl.pallas_call(
        prefix_kernel,
        out_shape=jax.ShapeDtypeStruct((full.shape[0], PREFIX), jnp.bfloat16),
        in_specs=[VMEM],
        out_specs=VMEM,
        compiler_params=params(),
        cost_estimate=pl.CostEstimate(flops=full.size * 8, bytes_accessed=4 << 20, transcendentals=0),
    )(full)


def maxima(tokens_ref, queries, best_ref, count, width):
    rows = queries.shape[0]
    step = min(256, rows)
    for at in range(0, rows, step):
        block = queries[at : at + step, :]
        for p in range(0, count, 2):
            scores = lax.dot_general(
                tokens_ref[p * width : (p + 2) * width, :],
                block,
                (((1,), (1,)), ((), ())),
                preferred_element_type=jnp.float32,
            )
            best_ref[p : p + 2, at : at + step] = jnp.max(scores.reshape(2, width, step), axis=1)


def select(chosen, values, contract):
    total = None
    for _ in range(3):
        term = values.astype(jnp.bfloat16)
        values = values - term.astype(jnp.float32)
        part = lax.dot_general(chosen, term, (contract, ((), ())), preferred_element_type=jnp.float32)
        total = part if total is None else total + part
    return total


def average(best, first, places, rows, me):
    qtok = best.shape[1] // places
    shape = (rows, best.shape[1])
    place = lax.broadcasted_iota(jnp.int32, shape, 1) // qtok + first
    row = lax.broadcasted_iota(jnp.int32, shape, 0)
    wanted = row + first if me is None else row ^ me
    chosen = jnp.where(place == wanted, 1.0 / qtok, 0.0).astype(jnp.bfloat16)
    return select(chosen, best[...], ((1,), (1,)))


def exact_kernel(tokens_ref, queries_ref, out_ref, best_ref):
    count, width = best_ref.shape[0], tokens_ref.shape[0] // best_ref.shape[0]
    places = out_ref.shape[0]
    maxima(tokens_ref, queries_ref[...], best_ref, count, width)
    out_ref[...] = average(best_ref, 0, places, places, None)


def coarse_kernel(first, places, after_ref, tokens_ref, queries_ref, *rest):
    out_ref, best_ref = rest[-2:]
    count, width = best_ref.shape[0], tokens_ref.shape[0] // best_ref.shape[0]
    maxima(tokens_ref, unit_prefix(queries_ref[...].astype(jnp.float32)), best_ref, count, width)
    result = average(best_ref, first, places, out_ref.shape[0], lax.axis_index("slab"))
    out_ref[...] = result if len(rest) == 2 else rest[0][...] + result


def score(kernel, rows, count, tokens, queries, after=(), partial=()):
    places, qtok, dim = queries.shape
    queries = queries.reshape(places * qtok, dim)
    return pl.pallas_call(
        kernel,
        out_shape=jax.ShapeDtypeStruct((rows, count), jnp.float32),
        in_specs=[ANY] * len(after) + [VMEM] * (2 + len(partial)),
        out_specs=VMEM,
        scratch_shapes=[pltpu.VMEM((count, places * qtok), jnp.float32)],
        compiler_params=params(),
        cost_estimate=pl.CostEstimate(
            flops=4 * tokens.shape[0] * places * qtok * 128, bytes_accessed=4 << 20, transcendentals=0
        ),
    )(*after, tokens, queries, *partial)


def pick_kernel(count, order, ids_ref, returned_ref, out_ref):
    ids = ids_ref[...]
    short = ids.shape[1]
    source = (ids // count) ^ lax.axis_index("slab")
    block, scale = jnp.zeros_like(ids), 1
    for low, size in reversed(order):
        block = block + ((source // low) % size) * scale
        scale *= size
    place = block * count + ids % count
    lanes = 128
    rows = returned_ref.shape[1] // lanes
    table = jnp.concatenate([returned_ref[:, r * lanes : (r + 1) * lanes] for r in range(rows)], axis=0)
    hot = lax.broadcasted_iota(jnp.int32, (lanes, short), 0) == place % lanes
    hot = jnp.where(hot, 1.0, 0.0).astype(jnp.bfloat16)
    column = None
    rest = table
    for _ in range(3):
        term = rest.astype(jnp.bfloat16)
        rest = rest - term.astype(jnp.float32)
        part = lax.dot_general(term, hot, (((1,), (0,)), ((), ())), preferred_element_type=jnp.float32)
        column = part if column is None else column + part
    mine = lax.broadcasted_iota(jnp.int32, (rows, short), 0) == place // lanes
    out_ref[...] = jnp.sum(jnp.where(mine, column, 0.0), axis=0, keepdims=True)


def exchange(array, offset, owners):
    return lax.ppermute(array, "slab", [(i, i ^ offset) for i in range(owners)])


def join(*parts):
    return jnp.concatenate(parts, axis=0)


def stages(owners):
    found, low = [], 1
    while low < owners:
        size = min(4, owners // low)
        found.append((low, size))
        low *= size
    return found


def per_device(queries, passages, lengths, shortlist):
    owners = lax.axis_size("slab")
    count = passages.shape[0]
    order = stages(owners)
    half = owners // 2
    held = queries
    full = near = far = kept = None
    for low, size in order:
        came = [exchange(held, low * k, owners) for k in range(1, size)]
        if low == 1:
            full = live_tokens(lengths, passages)
            came[-2], came[-1], full = lax.optimization_barrier((came[-2], came[-1], full))
        parts = [held] + came
        if low * size == owners:
            near = join(*parts[: size // 2])
            prefix = prefixes(full)
            kept = score(exact_kernel, half, count, full, near)
            parts[-1], kept, prefix = lax.optimization_barrier((parts[-1], kept, prefix))
            far = join(*parts[size // 2 :])
        else:
            held = join(*parts)
    sent = score(exact_kernel, half, count, full, far)
    coarse = None
    rows = join(kept, sent)
    for low, size in reversed(order):
        away = [exchange(rows[low * k : low * (k + 1)], low * k, owners) for k in reversed(range(1, size))]
        rows = jnp.concatenate([rows[:low]] + away[::-1], axis=1)
        if coarse is None:
            coarse = score(functools.partial(coarse_kernel, 0, half), owners, count, prefix, near, after=(sent,))
            coarse = score(
                functools.partial(coarse_kernel, half, half), owners, count, prefix, far, after=(sent,), partial=(coarse,)
            )
    picked = pl.pallas_call(
        functools.partial(pick_kernel, count, order),
        out_shape=jax.ShapeDtypeStruct(shortlist.shape, jnp.float32),
        in_specs=[VMEM, VMEM],
        out_specs=VMEM,
        compiler_params=params(),
    )(shortlist, rows)
    return (coarse.T, picked)


def solution(mesh):
    return jax.shard_map(
        per_device,
        mesh=mesh,
        in_specs=(
            P(("groups", "slab"), None, None),
            P(("groups", "slab"), None, None),
            P(("groups", "slab")),
            P(("groups", "slab"), None),
        ),
        out_specs=(P(("groups", "slab"), None), P(("groups", "slab"), None)),
        check_vma=False,
    )
```

```python
import functools

import jax
import jax.numpy as jnp
from jax import lax
from jax.experimental import pallas as pl
from jax.experimental.pallas import tpu as pltpu
from jax.sharding import PartitionSpec as P

PREFIX = 64
EPS = 1e-06
CHUNKS = 8
VMEM = pl.BlockSpec(memory_space=pltpu.VMEM)
ANY = pl.BlockSpec(memory_space=pl.ANY)
HBM = pl.BlockSpec(memory_space=pltpu.HBM)


def params(mib=16):
    return pltpu.CompilerParams(vmem_limit_bytes=mib << 20)


def unit_prefix(rows):
    head = rows[:, :PREFIX]
    total = jnp.sum(head * head, axis=-1, keepdims=True)
    return (head * lax.rsqrt(total + EPS)).astype(jnp.bfloat16)


def live_kernel(lens_hbm, passages_hbm, full_ref, lens_ref, passages_ref, sems):
    count, width, dim = passages_ref.shape
    size = count // CHUNKS
    lens_copy = pltpu.make_async_copy(lens_hbm, lens_ref, sems.at[CHUNKS])
    lens_copy.start()
    copies = []
    for c in range(CHUNKS):
        part = pl.ds(c * size, size)
        copies.append(pltpu.make_async_copy(passages_hbm.at[part], passages_ref.at[part], sems.at[c]))
        copies[-1].start()
    lens_copy.wait()
    row = lax.broadcasted_iota(jnp.int32, (width, dim), 0)
    for p in range(count):
        if p % size == 0:
            copies[p // size].wait()
        tokens = passages_ref[p].astype(jnp.float32)
        tokens = jnp.where(row < lens_ref[p], tokens, tokens[0:1])
        full_ref[pl.ds(p * width, width), :] = tokens.astype(jnp.bfloat16)


def live_tokens(lengths, passages):
    count, width, dim = passages.shape
    return pl.pallas_call(
        live_kernel,
        out_shape=jax.ShapeDtypeStruct((count * width, dim), jnp.bfloat16),
        in_specs=[HBM, HBM],
        out_specs=VMEM,
        scratch_shapes=[
            pltpu.SMEM((count,), jnp.int32),
            pltpu.VMEM((count, width, dim), jnp.bfloat16),
            pltpu.SemaphoreType.DMA((CHUNKS + 1,)),
        ],
        compiler_params=params(50),
        cost_estimate=pl.CostEstimate(flops=count * width * dim * 8, bytes_accessed=6 << 20, transcendentals=0),
    )(lengths, passages)


def prefix_kernel(full_ref, prefix_ref):
    width = 128
    for at in range(0, full_ref.shape[0], width):
        prefix_ref[at : at + width, :] = unit_prefix(full_ref[at : at + width, :].astype(jnp.float32))


def prefixes(full):
    return pl.pallas_call(
        prefix_kernel,
        out_shape=jax.ShapeDtypeStruct((full.shape[0], PREFIX), jnp.bfloat16),
        in_specs=[VMEM],
        out_specs=VMEM,
        compiler_params=params(),
        cost_estimate=pl.CostEstimate(flops=full.size * 8, bytes_accessed=4 << 20, transcendentals=0),
    )(full)


def maxima(tokens_ref, queries, best_ref, count, width):
    rows = queries.shape[0]
    step = min(256, rows)
    for at in range(0, rows, step):
        block = queries[at : at + step, :]
        for p in range(0, count, 2):
            scores = lax.dot_general(
                tokens_ref[p * width : (p + 2) * width, :],
                block,
                (((1,), (1,)), ((), ())),
                preferred_element_type=jnp.float32,
            )
            best_ref[p : p + 2, at : at + step] = jnp.max(scores.reshape(2, width, step), axis=1)


def select(chosen, values, contract):
    total = None
    for _ in range(3):
        term = values.astype(jnp.bfloat16)
        values = values - term.astype(jnp.float32)
        part = lax.dot_general(chosen, term, (contract, ((), ())), preferred_element_type=jnp.float32)
        total = part if total is None else total + part
    return total


def average(best, first, places, rows, whose=None):
    qtok = best.shape[1] // places
    shape = (rows, best.shape[1])
    place = lax.broadcasted_iota(jnp.int32, shape, 1) // qtok + first
    row = lax.broadcasted_iota(jnp.int32, shape, 0)
    hit = place == row + first if whose is None else whose(place) == row
    chosen = jnp.where(hit, 1.0 / qtok, 0.0).astype(jnp.bfloat16)
    return select(chosen, best[...], ((1,), (1,)))


def regroup(place, order):
    distance, below = jnp.zeros_like(place), 1
    for low, size in order:
        distance = distance + (place // below) % size * low
        below *= size
    return distance


def exact_kernel(tokens_ref, queries_ref, out_ref, best_ref):
    count, width = best_ref.shape[0], tokens_ref.shape[0] // best_ref.shape[0]
    places = out_ref.shape[0]
    maxima(tokens_ref, queries_ref[...], best_ref, count, width)
    out_ref[...] = average(best_ref, 0, places, places)


def coarse_kernel(order, first, places, after_ref, tokens_ref, queries_ref, *rest):
    out_ref, best_ref = rest[-2:]
    count, width = best_ref.shape[0], tokens_ref.shape[0] // best_ref.shape[0]
    maxima(tokens_ref, unit_prefix(queries_ref[...].astype(jnp.float32)), best_ref, count, width)

    def whose(place):
        return regroup(place, order) ^ lax.axis_index("slab")

    result = average(best_ref, first, places, out_ref.shape[0], whose)
    out_ref[...] = result if len(rest) == 2 else rest[0][...] + result


def score(kernel, rows, count, tokens, queries, after=(), partial=()):
    places, qtok, dim = queries.shape
    queries = queries.reshape(places * qtok, dim)
    return pl.pallas_call(
        kernel,
        out_shape=jax.ShapeDtypeStruct((rows, count), jnp.float32),
        in_specs=[ANY] * len(after) + [VMEM] * (2 + len(partial)),
        out_specs=VMEM,
        scratch_shapes=[pltpu.VMEM((count, places * qtok), jnp.float32)],
        compiler_params=params(),
        cost_estimate=pl.CostEstimate(
            flops=4 * tokens.shape[0] * places * qtok * 128, bytes_accessed=4 << 20, transcendentals=0
        ),
    )(*after, tokens, queries, *partial)


def pick_kernel(count, order, ids_ref, returned_ref, out_ref):
    ids = ids_ref[...]
    short = ids.shape[1]
    source = (ids // count) ^ lax.axis_index("slab")
    block, scale = jnp.zeros_like(ids), 1
    for low, size in reversed(order):
        block = block + ((source // low) % size) * scale
        scale *= size
    place = block * count + ids % count
    lanes = 128
    rows = returned_ref.shape[1] // lanes
    table = jnp.concatenate([returned_ref[:, r * lanes : (r + 1) * lanes] for r in range(rows)], axis=0)
    hot = lax.broadcasted_iota(jnp.int32, (lanes, short), 0) == place % lanes
    hot = jnp.where(hot, 1.0, 0.0).astype(jnp.bfloat16)
    column = None
    rest = table
    for _ in range(3):
        term = rest.astype(jnp.bfloat16)
        rest = rest - term.astype(jnp.float32)
        part = lax.dot_general(term, hot, (((1,), (0,)), ((), ())), preferred_element_type=jnp.float32)
        column = part if column is None else column + part
    mine = lax.broadcasted_iota(jnp.int32, (rows, short), 0) == place // lanes
    out_ref[...] = jnp.sum(jnp.where(mine, column, 0.0), axis=0, keepdims=True)


def exchange(array, offset, owners):
    return lax.ppermute(array, "slab", [(i, i ^ offset) for i in range(owners)])


def join(*parts):
    return jnp.concatenate(parts, axis=0)


def stages(owners):
    found, low = [], 1
    while low < owners:
        size = min(4, owners // low)
        found.append((low, size))
        low *= size
    return found[::-1]


def per_device(queries, passages, lengths, shortlist):
    owners = lax.axis_size("slab")
    count = passages.shape[0]
    order = stages(owners)
    half = owners // 2
    held = queries
    full = near = far = kept = None
    for low, size in order:
        came = [exchange(held, low * k, owners) for k in range(1, size)]
        parts = [held] + came
        if held is queries:
            full = live_tokens(lengths, passages)
            parts[-2], parts[-1], full = lax.optimization_barrier((parts[-2], parts[-1], full))
        if len(parts) * held.shape[0] == owners:
            near = join(*parts[: size // 2])
            prefix = prefixes(full)
            kept = score(exact_kernel, half, count, full, near)
            parts[-1], kept, prefix = lax.optimization_barrier((parts[-1], kept, prefix))
            far = join(*parts[size // 2 :])
        else:
            held = join(*parts)
    sent = score(exact_kernel, half, count, full, far)
    coarse = None
    rows = join(kept, sent)
    for low, size in reversed(order):
        group = rows.shape[0] // size
        away = [exchange(rows[group * k : group * (k + 1)], low * k, owners) for k in reversed(range(1, size))]
        rows = jnp.concatenate([rows[:group]] + away[::-1], axis=1)
        if coarse is None:
            near_kernel = functools.partial(coarse_kernel, order, 0, half)
            far_kernel = functools.partial(coarse_kernel, order, half, half)
            coarse = score(near_kernel, owners, count, prefix, near, after=(sent,))
            coarse = score(far_kernel, owners, count, prefix, far, after=(sent,), partial=(coarse,))
    picked = pl.pallas_call(
        functools.partial(pick_kernel, count, order),
        out_shape=jax.ShapeDtypeStruct(shortlist.shape, jnp.float32),
        in_specs=[VMEM, VMEM],
        out_specs=VMEM,
        compiler_params=params(),
    )(shortlist, rows)
    return (coarse.T, picked)


def solution(mesh):
    return jax.shard_map(
        per_device,
        mesh=mesh,
        in_specs=(
            P(("groups", "slab"), None, None),
            P(("groups", "slab"), None, None),
            P(("groups", "slab")),
            P(("groups", "slab"), None),
        ),
        out_specs=(P(("groups", "slab"), None), P(("groups", "slab"), None)),
        check_vma=False,
    )
```

```python
import functools

import jax
import jax.numpy as jnp
from jax import lax
from jax.experimental import pallas as pl
from jax.experimental.pallas import tpu as pltpu
from jax.sharding import PartitionSpec as P

PREFIX = 64
EPS = 1e-06
CHUNKS = 8
VMEM = pl.BlockSpec(memory_space=pltpu.VMEM)
ANY = pl.BlockSpec(memory_space=pl.ANY)
HBM = pl.BlockSpec(memory_space=pltpu.HBM)


def params(mib=16):
    return pltpu.CompilerParams(vmem_limit_bytes=mib << 20)


def unit_prefix(rows):
    head = rows[:, :PREFIX]
    total = jnp.sum(head * head, axis=-1, keepdims=True)
    return (head * lax.rsqrt(total + EPS)).astype(jnp.bfloat16)


def live_kernel(lens_hbm, passages_hbm, full_ref, lens_ref, passages_ref, sems):
    count, width, dim = passages_ref.shape
    size = count // CHUNKS
    lens_copy = pltpu.make_async_copy(lens_hbm, lens_ref, sems.at[CHUNKS])
    lens_copy.start()
    copies = []
    for c in range(CHUNKS):
        part = pl.ds(c * size, size)
        copies.append(pltpu.make_async_copy(passages_hbm.at[part], passages_ref.at[part], sems.at[c]))
        copies[-1].start()
    lens_copy.wait()
    row = lax.broadcasted_iota(jnp.int32, (width, dim), 0)
    for p in range(count):
        if p % size == 0:
            copies[p // size].wait()
        tokens = passages_ref[p].astype(jnp.float32)
        tokens = jnp.where(row < lens_ref[p], tokens, tokens[0:1])
        full_ref[pl.ds(p * width, width), :] = tokens.astype(jnp.bfloat16)


def live_tokens(lengths, passages):
    count, width, dim = passages.shape
    return pl.pallas_call(
        live_kernel,
        out_shape=jax.ShapeDtypeStruct((count * width, dim), jnp.bfloat16),
        in_specs=[HBM, HBM],
        out_specs=VMEM,
        scratch_shapes=[
            pltpu.SMEM((count,), jnp.int32),
            pltpu.VMEM((count, width, dim), jnp.bfloat16),
            pltpu.SemaphoreType.DMA((CHUNKS + 1,)),
        ],
        compiler_params=params(50),
        cost_estimate=pl.CostEstimate(flops=count * width * dim * 8, bytes_accessed=6 << 20, transcendentals=0),
    )(lengths, passages)


def prefix_kernel(*refs):
    full_ref, prefix_ref = refs[-2:]
    width = 128
    for at in range(0, full_ref.shape[0], width):
        prefix_ref[at : at + width, :] = unit_prefix(full_ref[at : at + width, :].astype(jnp.float32))


def prefixes(after, full):
    return pl.pallas_call(
        prefix_kernel,
        out_shape=jax.ShapeDtypeStruct((full.shape[0], PREFIX), jnp.bfloat16),
        in_specs=[ANY] * len(after) + [VMEM],
        out_specs=VMEM,
        compiler_params=params(),
        cost_estimate=pl.CostEstimate(flops=full.size * 8, bytes_accessed=4 << 20, transcendentals=0),
    )(*after, full)


def maxima(tokens_ref, queries, best_ref, count, width):
    rows = queries.shape[0]
    for at in range(0, rows, 256):
        block = queries[at : at + 256, :]
        step = block.shape[0]
        for p in range(0, count, 2):
            scores = lax.dot_general(
                tokens_ref[p * width : (p + 2) * width, :],
                block,
                (((1,), (1,)), ((), ())),
                preferred_element_type=jnp.float32,
            )
            best_ref[p : p + 2, at : at + step] = jnp.max(scores.reshape(2, width, step), axis=1)


def select(chosen, values, contract):
    total = None
    for _ in range(3):
        term = values.astype(jnp.bfloat16)
        values = values - term.astype(jnp.float32)
        part = lax.dot_general(chosen, term, (contract, ((), ())), preferred_element_type=jnp.float32)
        total = part if total is None else total + part
    return total


def average(best, first, places, rows, whose=None):
    qtok = best.shape[1] // places
    shape = (rows, best.shape[1])
    place = lax.broadcasted_iota(jnp.int32, shape, 1) // qtok + first
    row = lax.broadcasted_iota(jnp.int32, shape, 0)
    hit = place == row + first if whose is None else whose(place) == row
    chosen = jnp.where(hit, 1.0 / qtok, 0.0).astype(jnp.bfloat16)
    return select(chosen, best[...], ((1,), (1,)))


def regroup(place, order):
    distance, below = jnp.zeros_like(place), 1
    for low, size in order:
        distance = distance + (place // below) % size * low
        below *= size
    return distance


def exact_kernel(tokens_ref, queries_ref, out_ref, best_ref):
    count, width = best_ref.shape[0], tokens_ref.shape[0] // best_ref.shape[0]
    places = out_ref.shape[0]
    maxima(tokens_ref, queries_ref[...], best_ref, count, width)
    out_ref[...] = average(best_ref, 0, places, places)


def coarse_kernel(order, first, places, after_ref, tokens_ref, queries_ref, *rest):
    out_ref, best_ref = rest[-2:]
    count, width = best_ref.shape[0], tokens_ref.shape[0] // best_ref.shape[0]
    maxima(tokens_ref, unit_prefix(queries_ref[...].astype(jnp.float32)), best_ref, count, width)

    def whose(place):
        return regroup(place, order) ^ lax.axis_index("slab")

    result = average(best_ref, first, places, out_ref.shape[0], whose)
    out_ref[...] = result if len(rest) == 2 else rest[0][...] + result


def score(kernel, rows, count, tokens, queries, after=(), partial=()):
    places, qtok, dim = queries.shape
    queries = queries.reshape(places * qtok, dim)
    return pl.pallas_call(
        kernel,
        out_shape=jax.ShapeDtypeStruct((rows, count), jnp.float32),
        in_specs=[ANY] * len(after) + [VMEM] * (2 + len(partial)),
        out_specs=VMEM,
        scratch_shapes=[pltpu.VMEM((count, places * qtok), jnp.float32)],
        compiler_params=params(),
        cost_estimate=pl.CostEstimate(
            flops=4 * tokens.shape[0] * places * qtok * 128, bytes_accessed=4 << 20, transcendentals=0
        ),
    )(*after, tokens, queries, *partial)


def pick_kernel(count, order, ids_ref, returned_ref, out_ref):
    ids = ids_ref[...]
    short = ids.shape[1]
    source = (ids // count) ^ lax.axis_index("slab")
    block, scale = jnp.zeros_like(ids), 1
    for low, size in reversed(order):
        block = block + ((source // low) % size) * scale
        scale *= size
    place = block * count + ids % count
    lanes = 128
    rows = returned_ref.shape[1] // lanes
    table = jnp.concatenate([returned_ref[:, r * lanes : (r + 1) * lanes] for r in range(rows)], axis=0)
    hot = lax.broadcasted_iota(jnp.int32, (lanes, short), 0) == place % lanes
    hot = jnp.where(hot, 1.0, 0.0).astype(jnp.bfloat16)
    column = None
    rest = table
    for _ in range(3):
        term = rest.astype(jnp.bfloat16)
        rest = rest - term.astype(jnp.float32)
        part = lax.dot_general(term, hot, (((1,), (0,)), ((), ())), preferred_element_type=jnp.float32)
        column = part if column is None else column + part
    mine = lax.broadcasted_iota(jnp.int32, (rows, short), 0) == place // lanes
    out_ref[...] = jnp.sum(jnp.where(mine, column, 0.0), axis=0, keepdims=True)


def exchange(array, offset, owners):
    return lax.ppermute(array, "slab", [(i, i ^ offset) for i in range(owners)])


def join(*parts):
    return jnp.concatenate(parts, axis=0)


def stages(owners):
    found, low = [], 1
    while low < owners:
        size = min(4, owners // low)
        found.append((low, size))
        low *= size
    return found[::-1]


def per_device(queries, passages, lengths, shortlist):
    owners = lax.axis_size("slab")
    count = passages.shape[0]
    order = stages(owners)
    half = owners // 2
    held = queries
    full = None
    for low, size in order:
        came = [exchange(held, low * k, owners) for k in range(1, size)]
        parts = [held] + came
        if held is queries:
            full = live_tokens(lengths, passages)
            parts[-2], parts[-1], full = lax.optimization_barrier((parts[-2], parts[-1], full))
        if len(parts) * held.shape[0] < owners:
            held = join(*parts)
    scores = [score(exact_kernel, half, count, full, join(*parts[: size // 2]))]
    for part in parts[size // 2 :]:
        scores.append(score(exact_kernel, part.shape[0], count, full, part))
    coarse = None
    rows = join(*scores)
    for low, size in reversed(order):
        group = rows.shape[0] // size
        away = [exchange(rows[group * k : group * (k + 1)], low * k, owners) for k in reversed(range(1, size))]
        rows = jnp.concatenate([rows[:group]] + away[::-1], axis=1)
        if coarse is None:
            prefix = prefixes(scores, full)
            near_kernel = functools.partial(coarse_kernel, order, 0, held.shape[0])
            far_kernel = functools.partial(coarse_kernel, order, held.shape[0], owners - held.shape[0])
            coarse = score(near_kernel, owners, count, prefix, held, after=(scores[-1],))
            coarse = score(far_kernel, owners, count, prefix, join(*came), after=(scores[-1],), partial=(coarse,))
    picked = pl.pallas_call(
        functools.partial(pick_kernel, count, order),
        out_shape=jax.ShapeDtypeStruct(shortlist.shape, jnp.float32),
        in_specs=[VMEM, VMEM],
        out_specs=VMEM,
        compiler_params=params(),
    )(shortlist, rows)
    return (coarse.T, picked)


def solution(mesh):
    return jax.shard_map(
        per_device,
        mesh=mesh,
        in_specs=(
            P(("groups", "slab"), None, None),
            P(("groups", "slab"), None, None),
            P(("groups", "slab")),
            P(("groups", "slab"), None),
        ),
        out_specs=(P(("groups", "slab"), None), P(("groups", "slab"), None)),
        check_vma=False,
    )
```

```python
import functools

import jax
import jax.numpy as jnp
from jax import lax
from jax.experimental import pallas as pl
from jax.experimental.pallas import tpu as pltpu
from jax.sharding import PartitionSpec as P

PREFIX = 64
EPS = 1e-06
CHUNKS = 8
VMEM = pl.BlockSpec(memory_space=pltpu.VMEM)
ANY = pl.BlockSpec(memory_space=pl.ANY)
HBM = pl.BlockSpec(memory_space=pltpu.HBM)


def params(mib=16):
    return pltpu.CompilerParams(vmem_limit_bytes=mib << 20)


def unit_prefix(rows):
    head = rows[:, :PREFIX]
    total = jnp.sum(head * head, axis=-1, keepdims=True)
    return (head * lax.rsqrt(total + EPS)).astype(jnp.bfloat16)


def live_kernel(lens_hbm, passages_hbm, full_ref, lens_ref, passages_ref, sems):
    count, width, dim = passages_ref.shape
    size = count // CHUNKS
    lens_copy = pltpu.make_async_copy(lens_hbm, lens_ref, sems.at[CHUNKS])
    lens_copy.start()
    copies = []
    for c in range(CHUNKS):
        part = pl.ds(c * size, size)
        copies.append(pltpu.make_async_copy(passages_hbm.at[part], passages_ref.at[part], sems.at[c]))
        copies[-1].start()
    lens_copy.wait()
    row = lax.broadcasted_iota(jnp.int32, (width, dim), 0)
    for p in range(count):
        if p % size == 0:
            copies[p // size].wait()
        tokens = passages_ref[p].astype(jnp.float32)
        tokens = jnp.where(row < lens_ref[p], tokens, tokens[0:1])
        full_ref[pl.ds(p * width, width), :] = tokens.astype(jnp.bfloat16)


def live_tokens(lengths, passages):
    count, width, dim = passages.shape
    return pl.pallas_call(
        live_kernel,
        out_shape=jax.ShapeDtypeStruct((count * width, dim), jnp.bfloat16),
        in_specs=[HBM, HBM],
        out_specs=VMEM,
        scratch_shapes=[
            pltpu.SMEM((count,), jnp.int32),
            pltpu.VMEM((count, width, dim), jnp.bfloat16),
            pltpu.SemaphoreType.DMA((CHUNKS + 1,)),
        ],
        compiler_params=params(50),
        cost_estimate=pl.CostEstimate(flops=count * width * dim * 8, bytes_accessed=6 << 20, transcendentals=0),
    )(lengths, passages)


def prefix_kernel(*refs):
    full_ref, prefix_ref = refs[-2:]
    width = 128
    for at in range(0, full_ref.shape[0], width):
        prefix_ref[at : at + width, :] = unit_prefix(full_ref[at : at + width, :].astype(jnp.float32))


def prefixes(after, full):
    return pl.pallas_call(
        prefix_kernel,
        out_shape=jax.ShapeDtypeStruct((full.shape[0], PREFIX), jnp.bfloat16),
        in_specs=[ANY] * len(after) + [VMEM],
        out_specs=VMEM,
        compiler_params=params(),
        cost_estimate=pl.CostEstimate(flops=full.size * 8, bytes_accessed=4 << 20, transcendentals=0),
    )(*after, full)


def maxima(tokens_ref, queries, best_ref, count, width):
    rows = queries.shape[0]
    for at in range(0, rows, 256):
        block = queries[at : at + 256, :]
        step = block.shape[0]
        for p in range(0, count, 2):
            scores = lax.dot_general(
                tokens_ref[p * width : (p + 2) * width, :],
                block,
                (((1,), (1,)), ((), ())),
                preferred_element_type=jnp.float32,
            )
            best_ref[p : p + 2, at : at + step] = jnp.max(scores.reshape(2, width, step), axis=1)


def select(chosen, values, contract):
    total = None
    for _ in range(3):
        term = values.astype(jnp.bfloat16)
        values = values - term.astype(jnp.float32)
        part = lax.dot_general(chosen, term, (contract, ((), ())), preferred_element_type=jnp.float32)
        total = part if total is None else total + part
    return total


def average(best, first, places, rows, whose=None):
    qtok = best.shape[1] // places
    shape = (rows, best.shape[1])
    place = lax.broadcasted_iota(jnp.int32, shape, 1) // qtok + first
    row = lax.broadcasted_iota(jnp.int32, shape, 0)
    hit = place == row + first if whose is None else whose(place) == row
    chosen = jnp.where(hit, 1.0 / qtok, 0.0).astype(jnp.bfloat16)
    return select(chosen, best[...], ((1,), (1,)))


def regroup(place, order):
    distance, below = jnp.zeros_like(place), 1
    for low, size in order:
        distance = distance + (place // below) % size * low
        below *= size
    return distance


def exact_kernel(tokens_ref, queries_ref, out_ref, best_ref):
    count, width = best_ref.shape[0], tokens_ref.shape[0] // best_ref.shape[0]
    places = out_ref.shape[0]
    maxima(tokens_ref, queries_ref[...], best_ref, count, width)
    out_ref[...] = average(best_ref, 0, places, places)


def coarse_kernel(order, first, places, after_ref, tokens_ref, queries_ref, *rest):
    out_ref, best_ref = rest[-2:]
    count, width = best_ref.shape[0], tokens_ref.shape[0] // best_ref.shape[0]
    maxima(tokens_ref, unit_prefix(queries_ref[...].astype(jnp.float32)), best_ref, count, width)

    def whose(place):
        return regroup(place, order) ^ lax.axis_index("slab")

    result = average(best_ref, first, places, out_ref.shape[0], whose)
    out_ref[...] = result if len(rest) == 2 else rest[0][...] + result


def score(kernel, rows, count, tokens, queries, after=(), partial=()):
    places, qtok, dim = queries.shape
    queries = queries.reshape(places * qtok, dim)
    return pl.pallas_call(
        kernel,
        out_shape=jax.ShapeDtypeStruct((rows, count), jnp.float32),
        in_specs=[ANY] * len(after) + [VMEM] * (2 + len(partial)),
        out_specs=VMEM,
        scratch_shapes=[pltpu.VMEM((count, places * qtok), jnp.float32)],
        compiler_params=params(),
        cost_estimate=pl.CostEstimate(
            flops=4 * tokens.shape[0] * places * qtok * 128, bytes_accessed=4 << 20, transcendentals=0
        ),
    )(*after, tokens, queries, *partial)


def pick_kernel(count, order, coarse_ref, ids_ref, returned_ref, exact_out, coarse_out, picked_ref, sems):
    coarse_copy = pltpu.make_async_copy(coarse_ref, coarse_out, sems.at[0])
    exact_copy = pltpu.make_async_copy(picked_ref, exact_out, sems.at[1])
    coarse_copy.start()
    ids = ids_ref[...]
    short = ids.shape[1]
    source = (ids // count) ^ lax.axis_index("slab")
    block, scale = jnp.zeros_like(ids), 1
    for low, size in reversed(order):
        block = block + ((source // low) % size) * scale
        scale *= size
    place = block * count + ids % count
    lanes = 128
    rows = returned_ref.shape[1] // lanes
    table = jnp.concatenate([returned_ref[:, r * lanes : (r + 1) * lanes] for r in range(rows)], axis=0)
    hot = lax.broadcasted_iota(jnp.int32, (lanes, short), 0) == place % lanes
    hot = jnp.where(hot, 1.0, 0.0).astype(jnp.bfloat16)
    column = None
    rest = table
    for _ in range(3):
        term = rest.astype(jnp.bfloat16)
        rest = rest - term.astype(jnp.float32)
        part = lax.dot_general(term, hot, (((1,), (0,)), ((), ())), preferred_element_type=jnp.float32)
        column = part if column is None else column + part
    mine = lax.broadcasted_iota(jnp.int32, (rows, short), 0) == place // lanes
    picked_ref[...] = jnp.sum(jnp.where(mine, column, 0.0), axis=0, keepdims=True)
    exact_copy.start()
    coarse_copy.wait()
    exact_copy.wait()


def exchange(array, offset, owners):
    return lax.ppermute(array, "slab", [(i, i ^ offset) for i in range(owners)])


def join(*parts):
    return jnp.concatenate(parts, axis=0)


def stages(owners):
    found, low = [], 1
    while low < owners:
        size = min(4, owners // low)
        found.append((low, size))
        low *= size
    return found[::-1]


def per_device(queries, passages, lengths, shortlist):
    owners = lax.axis_size("slab")
    count = passages.shape[0]
    order = stages(owners)
    half = owners // 2
    held = queries
    full = None
    for low, size in order:
        came = [exchange(held, low * k, owners) for k in range(1, size)]
        parts = [held] + came
        if held is queries:
            full = live_tokens(lengths, passages)
            parts[-2], parts[-1], full = lax.optimization_barrier((parts[-2], parts[-1], full))
        if len(parts) * held.shape[0] < owners:
            held = join(*parts)
    scores = [score(exact_kernel, half, count, full, join(*parts[: size // 2]))]
    for part in parts[size // 2 :]:
        scores.append(score(exact_kernel, part.shape[0], count, full, part))
    coarse = None
    rows = join(*scores)
    for low, size in reversed(order):
        group = rows.shape[0] // size
        away = [exchange(rows[group * k : group * (k + 1)], low * k, owners) for k in reversed(range(1, size))]
        rows = jnp.concatenate([rows[:group]] + away[::-1], axis=1)
        if coarse is None:
            prefix = prefixes(scores, full)
            near_kernel = functools.partial(coarse_kernel, order, 0, held.shape[0])
            far_kernel = functools.partial(coarse_kernel, order, held.shape[0], owners - held.shape[0])
            coarse = score(near_kernel, owners, count, prefix, held, after=(scores[-1],))
            coarse = score(far_kernel, owners, count, prefix, join(*came), after=(scores[-1],), partial=(coarse,))
    exact, coarse = pl.pallas_call(
        functools.partial(pick_kernel, count, order),
        out_shape=(
            jax.ShapeDtypeStruct(shortlist.shape, jnp.float32),
            jax.ShapeDtypeStruct(coarse.shape, jnp.float32),
        ),
        in_specs=[VMEM, VMEM, VMEM],
        out_specs=(ANY, ANY),
        scratch_shapes=[pltpu.VMEM(shortlist.shape, jnp.float32), pltpu.SemaphoreType.DMA((2,))],
        compiler_params=params(),
    )(coarse, shortlist, rows)
    return (coarse.T, exact)


def solution(mesh):
    return jax.shard_map(
        per_device,
        mesh=mesh,
        in_specs=(
            P(("groups", "slab"), None, None),
            P(("groups", "slab"), None, None),
            P(("groups", "slab")),
            P(("groups", "slab"), None),
        ),
        out_specs=(P(("groups", "slab"), None), P(("groups", "slab"), None)),
        check_vma=False,
    )
```

```python
import functools

import jax
import jax.numpy as jnp
from jax import lax
from jax.experimental import pallas as pl
from jax.experimental.pallas import tpu as pltpu
from jax.sharding import PartitionSpec as P

PREFIX = 64
EPS = 1e-06
CHUNKS = 8
VMEM = pl.BlockSpec(memory_space=pltpu.VMEM)
ANY = pl.BlockSpec(memory_space=pl.ANY)
HBM = pl.BlockSpec(memory_space=pltpu.HBM)


def params(mib=16):
    return pltpu.CompilerParams(vmem_limit_bytes=mib << 20)


def unit_prefix(rows):
    head = rows[:, :PREFIX]
    total = jnp.sum(head * head, axis=-1, keepdims=True)
    return (head * lax.rsqrt(total + EPS)).astype(jnp.bfloat16)


def live_kernel(lens_hbm, passages_hbm, full_ref, lens_ref, passages_ref, sems):
    count, width, dim = passages_ref.shape
    size = count // CHUNKS
    lens_copy = pltpu.make_async_copy(lens_hbm, lens_ref, sems.at[CHUNKS])
    lens_copy.start()
    copies = []
    for c in range(CHUNKS):
        part = pl.ds(c * size, size)
        copies.append(pltpu.make_async_copy(passages_hbm.at[part], passages_ref.at[part], sems.at[c]))
        copies[-1].start()
    lens_copy.wait()
    row = lax.broadcasted_iota(jnp.int32, (width, dim), 0)
    for p in range(count):
        if p % size == 0:
            copies[p // size].wait()
        tokens = passages_ref[p].astype(jnp.float32)
        tokens = jnp.where(row < lens_ref[p], tokens, tokens[0:1])
        full_ref[pl.ds(p * width, width), :] = tokens.astype(jnp.bfloat16)


def live_tokens(lengths, passages):
    count, width, dim = passages.shape
    return pl.pallas_call(
        live_kernel,
        out_shape=jax.ShapeDtypeStruct((count * width, dim), jnp.bfloat16),
        in_specs=[HBM, HBM],
        out_specs=VMEM,
        scratch_shapes=[
            pltpu.SMEM((count,), jnp.int32),
            pltpu.VMEM((count, width, dim), jnp.bfloat16),
            pltpu.SemaphoreType.DMA((CHUNKS + 1,)),
        ],
        compiler_params=params(50),
        cost_estimate=pl.CostEstimate(flops=count * width * dim * 8, bytes_accessed=6 << 20, transcendentals=0),
    )(lengths, passages)


def prefix_kernel(*refs):
    full_ref, prefix_ref = refs[-2:]
    width = 128
    for at in range(0, full_ref.shape[0], width):
        prefix_ref[at : at + width, :] = unit_prefix(full_ref[at : at + width, :].astype(jnp.float32))


def prefixes(after, full):
    return pl.pallas_call(
        prefix_kernel,
        out_shape=jax.ShapeDtypeStruct((full.shape[0], PREFIX), jnp.bfloat16),
        in_specs=[ANY] * len(after) + [VMEM],
        out_specs=VMEM,
        compiler_params=params(),
        cost_estimate=pl.CostEstimate(flops=full.size * 8, bytes_accessed=4 << 20, transcendentals=0),
    )(*after, full)


def maxima(tokens_ref, queries, best_ref, count, width):
    rows = queries.shape[0]
    for at in range(0, rows, 256):
        block = queries[at : at + 256, :]
        step = block.shape[0]
        for p in range(0, count, 2):
            scores = lax.dot_general(
                tokens_ref[p * width : (p + 2) * width, :],
                block,
                (((1,), (1,)), ((), ())),
                preferred_element_type=jnp.float32,
            )
            best_ref[p : p + 2, at : at + step] = jnp.max(scores.reshape(2, width, step), axis=1)


def select(chosen, values, contract):
    total = None
    for _ in range(3):
        term = values.astype(jnp.bfloat16)
        values = values - term.astype(jnp.float32)
        part = lax.dot_general(chosen, term, (contract, ((), ())), preferred_element_type=jnp.float32)
        total = part if total is None else total + part
    return total


def average(best, first, places, rows, whose=None):
    qtok = best.shape[1] // places
    shape = (rows, best.shape[1])
    place = lax.broadcasted_iota(jnp.int32, shape, 1) // qtok + first
    row = lax.broadcasted_iota(jnp.int32, shape, 0)
    hit = place == row + first if whose is None else whose(place) == row
    chosen = jnp.where(hit, 1.0 / qtok, 0.0).astype(jnp.bfloat16)
    return select(chosen, best[...], ((1,), (1,)))


def regroup(place, order):
    distance, below = jnp.zeros_like(place), 1
    for low, size in order:
        distance = distance + (place // below) % size * low
        below *= size
    return distance


def exact_kernel(tokens_ref, queries_ref, out_ref, best_ref):
    count, width = best_ref.shape[0], tokens_ref.shape[0] // best_ref.shape[0]
    places = out_ref.shape[0]
    maxima(tokens_ref, queries_ref[...], best_ref, count, width)
    out_ref[...] = average(best_ref, 0, places, places)


def coarse_kernel(order, first, places, *refs):
    tokens_ref, queries_ref, *rest = refs if first else refs[1:]
    out_ref, best_ref = rest[-2:]
    count, width = best_ref.shape[0], tokens_ref.shape[0] // best_ref.shape[0]
    maxima(tokens_ref, unit_prefix(queries_ref[...].astype(jnp.float32)), best_ref, count, width)

    def whose(place):
        return regroup(place, order) ^ lax.axis_index("slab")

    result = average(best_ref, first, places, out_ref.shape[0], whose)
    out_ref[...] = result if len(rest) == 2 else rest[0][...] + result


def score(kernel, rows, count, tokens, queries, after=(), partial=()):
    places, qtok, dim = queries.shape
    queries = queries.reshape(places * qtok, dim)
    return pl.pallas_call(
        kernel,
        out_shape=jax.ShapeDtypeStruct((rows, count), jnp.float32),
        in_specs=[ANY] * len(after) + [VMEM] * (2 + len(partial)),
        out_specs=VMEM,
        scratch_shapes=[pltpu.VMEM((count, places * qtok), jnp.float32)],
        compiler_params=params(),
        cost_estimate=pl.CostEstimate(
            flops=4 * tokens.shape[0] * places * qtok * 128, bytes_accessed=4 << 20, transcendentals=0
        ),
    )(*after, tokens, queries, *partial)


def pick_kernel(count, order, coarse_ref, ids_ref, returned_ref, exact_out, coarse_out, picked_ref, sems):
    coarse_copy = pltpu.make_async_copy(coarse_ref, coarse_out, sems.at[0])
    exact_copy = pltpu.make_async_copy(picked_ref, exact_out, sems.at[1])
    coarse_copy.start()
    ids = ids_ref[...]
    short = ids.shape[1]
    source = (ids // count) ^ lax.axis_index("slab")
    block, scale = jnp.zeros_like(ids), 1
    for low, size in reversed(order):
        block = block + ((source // low) % size) * scale
        scale *= size
    place = block * count + ids % count
    lanes = 128
    rows = returned_ref.shape[1] // lanes
    table = jnp.concatenate([returned_ref[:, r * lanes : (r + 1) * lanes] for r in range(rows)], axis=0)
    hot = lax.broadcasted_iota(jnp.int32, (lanes, short), 0) == place % lanes
    hot = jnp.where(hot, 1.0, 0.0).astype(jnp.bfloat16)
    column = None
    rest = table
    for _ in range(3):
        term = rest.astype(jnp.bfloat16)
        rest = rest - term.astype(jnp.float32)
        part = lax.dot_general(term, hot, (((1,), (0,)), ((), ())), preferred_element_type=jnp.float32)
        column = part if column is None else column + part
    mine = lax.broadcasted_iota(jnp.int32, (rows, short), 0) == place // lanes
    picked_ref[...] = jnp.sum(jnp.where(mine, column, 0.0), axis=0, keepdims=True)
    exact_copy.start()
    coarse_copy.wait()
    exact_copy.wait()


def exchange(array, offset, owners):
    return lax.ppermute(array, "slab", [(i, i ^ offset) for i in range(owners)])


def join(*parts):
    return jnp.concatenate(parts, axis=0)


def stages(owners):
    found, low = [], 1
    while low < owners:
        size = min(4, owners // low)
        found.append((low, size))
        low *= size
    return found[::-1]


def per_device(queries, passages, lengths, shortlist):
    owners = lax.axis_size("slab")
    count = passages.shape[0]
    order = stages(owners)
    half = owners // 2
    held = queries
    full = None
    for low, size in order:
        came = [exchange(held, low * k, owners) for k in range(1, size)]
        parts = [held] + came
        if held is queries:
            full = live_tokens(lengths, passages)
            parts[-2], parts[-1], full = lax.optimization_barrier((parts[-2], parts[-1], full))
        if len(parts) * held.shape[0] < owners:
            held = join(*parts)
    scores = [score(exact_kernel, half, count, full, join(*parts[: size // 2]))]
    for part in parts[size // 2 :]:
        scores.append(score(exact_kernel, part.shape[0], count, full, part))
    coarse = None
    rows = join(*scores)
    for low, size in reversed(order):
        group = rows.shape[0] // size
        away = [exchange(rows[group * k : group * (k + 1)], low * k, owners) for k in reversed(range(1, size))]
        rows = jnp.concatenate([rows[:group]] + away[::-1], axis=1)
        if coarse is None:
            prefix = prefixes(scores, full)
            near_kernel = functools.partial(coarse_kernel, order, 0, held.shape[0])
            far_kernel = functools.partial(coarse_kernel, order, held.shape[0], owners - held.shape[0])
            coarse = score(near_kernel, owners, count, prefix, held, after=(scores[-1],))
            coarse = score(far_kernel, owners, count, prefix, join(*came), partial=(coarse,))
    exact, coarse = pl.pallas_call(
        functools.partial(pick_kernel, count, order),
        out_shape=(
            jax.ShapeDtypeStruct(shortlist.shape, jnp.float32),
            jax.ShapeDtypeStruct(coarse.shape, jnp.float32),
        ),
        in_specs=[VMEM, VMEM, VMEM],
        out_specs=(ANY, ANY),
        scratch_shapes=[pltpu.VMEM(shortlist.shape, jnp.float32), pltpu.SemaphoreType.DMA((2,))],
        compiler_params=params(),
    )(coarse, shortlist, rows)
    return (coarse.T, exact)


def solution(mesh):
    return jax.shard_map(
        per_device,
        mesh=mesh,
        in_specs=(
            P(("groups", "slab"), None, None),
            P(("groups", "slab"), None, None),
            P(("groups", "slab")),
            P(("groups", "slab"), None),
        ),
        out_specs=(P(("groups", "slab"), None), P(("groups", "slab"), None)),
        check_vma=False,
    )
```

```python
import functools

import jax
import jax.numpy as jnp
from jax import lax
from jax.experimental import pallas as pl
from jax.experimental.pallas import tpu as pltpu
from jax.sharding import PartitionSpec as P

PREFIX = 64
EPS = 1e-06
CHUNKS = 8
VMEM = pl.BlockSpec(memory_space=pltpu.VMEM)
ANY = pl.BlockSpec(memory_space=pl.ANY)
HBM = pl.BlockSpec(memory_space=pltpu.HBM)


def params(mib=16):
    return pltpu.CompilerParams(vmem_limit_bytes=mib << 20)


def unit_prefix(rows):
    head = rows[:, :PREFIX]
    total = jnp.sum(head * head, axis=-1, keepdims=True)
    return (head * lax.rsqrt(total + EPS)).astype(jnp.bfloat16)


def live_kernel(lens_hbm, passages_hbm, full_ref, lens_ref, passages_ref, sems):
    count, width, dim = passages_ref.shape
    size = count // CHUNKS
    lens_copy = pltpu.make_async_copy(lens_hbm, lens_ref, sems.at[CHUNKS])
    lens_copy.start()
    copies = []
    for c in range(CHUNKS):
        part = pl.ds(c * size, size)
        copies.append(pltpu.make_async_copy(passages_hbm.at[part], passages_ref.at[part], sems.at[c]))
        copies[-1].start()
    lens_copy.wait()
    row = lax.broadcasted_iota(jnp.int32, (width, dim), 0)
    for p in range(count):
        if p % size == 0:
            copies[p // size].wait()
        tokens = passages_ref[p].astype(jnp.float32)
        tokens = jnp.where(row < lens_ref[p], tokens, tokens[0:1])
        full_ref[pl.ds(p * width, width), :] = tokens.astype(jnp.bfloat16)


def live_tokens(lengths, passages):
    count, width, dim = passages.shape
    return pl.pallas_call(
        live_kernel,
        out_shape=jax.ShapeDtypeStruct((count * width, dim), jnp.bfloat16),
        in_specs=[HBM, HBM],
        out_specs=VMEM,
        scratch_shapes=[
            pltpu.SMEM((count,), jnp.int32),
            pltpu.VMEM((count, width, dim), jnp.bfloat16),
            pltpu.SemaphoreType.DMA((CHUNKS + 1,)),
        ],
        compiler_params=params(50),
        cost_estimate=pl.CostEstimate(flops=count * width * dim * 8, bytes_accessed=6 << 20, transcendentals=0),
    )(lengths, passages)


def maxima(tokens_ref, queries, best_ref, count, width, prefix_ref=None):
    rows = queries.shape[0]
    for at in range(0, rows, 256):
        block = queries[at : at + 256, :]
        step = block.shape[0]
        for p in range(0, count, 2):
            tokens = (tokens_ref if prefix_ref is None or at == 0 else prefix_ref)[p * width : (p + 2) * width, :]
            if prefix_ref is not None and at == 0:
                tokens = unit_prefix(tokens.astype(jnp.float32))
                prefix_ref[p * width : (p + 2) * width, :] = tokens
            scores = lax.dot_general(
                tokens,
                block,
                (((1,), (1,)), ((), ())),
                preferred_element_type=jnp.float32,
            )
            best_ref[p : p + 2, at : at + step] = jnp.max(scores.reshape(2, width, step), axis=1)


def select(chosen, values, contract):
    total = None
    for _ in range(3):
        term = values.astype(jnp.bfloat16)
        values = values - term.astype(jnp.float32)
        part = lax.dot_general(chosen, term, (contract, ((), ())), preferred_element_type=jnp.float32)
        total = part if total is None else total + part
    return total


def average(best, first, places, rows, whose=None):
    qtok = best.shape[1] // places
    shape = (rows, best.shape[1])
    place = lax.broadcasted_iota(jnp.int32, shape, 1) // qtok + first
    row = lax.broadcasted_iota(jnp.int32, shape, 0)
    hit = place == row + first if whose is None else whose(place) == row
    chosen = jnp.where(hit, 1.0 / qtok, 0.0).astype(jnp.bfloat16)
    return select(chosen, best[...], ((1,), (1,)))


def regroup(place, order):
    distance, below = jnp.zeros_like(place), 1
    for low, size in order:
        distance = distance + (place // below) % size * low
        below *= size
    return distance


def exact_kernel(tokens_ref, queries_ref, out_ref, best_ref):
    count, width = best_ref.shape[0], tokens_ref.shape[0] // best_ref.shape[0]
    places = out_ref.shape[0]
    maxima(tokens_ref, queries_ref[...], best_ref, count, width)
    out_ref[...] = average(best_ref, 0, places, places)


def coarse(order, first, places, tokens_ref, queries_ref, best_ref, owners, *prefix):
    def whose(place):
        return regroup(place, order) ^ lax.axis_index("slab")

    count, width = best_ref.shape[0], tokens_ref.shape[0] // best_ref.shape[0]
    maxima(tokens_ref, unit_prefix(queries_ref[...].astype(jnp.float32)), best_ref, count, width, *prefix)
    return average(best_ref, first, places, owners, whose)


def near_coarse_kernel(order, places, *refs):
    full_ref, queries_ref, out_ref, prefix_ref, best_ref = refs[-5:]
    out_ref[...] = coarse(order, 0, places, full_ref, queries_ref, best_ref, out_ref.shape[0], prefix_ref)


def far_coarse_kernel(order, first, places, tokens_ref, queries_ref, partial_ref, out_ref, best_ref):
    out_ref[...] = partial_ref[...] + coarse(order, first, places, tokens_ref, queries_ref, best_ref, out_ref.shape[0])


def score(kernel, rows, count, tokens, queries, after=(), partial=(), prefix=False):
    places, qtok, dim = queries.shape
    queries = queries.reshape(places * qtok, dim)
    shapes = [jax.ShapeDtypeStruct((rows, count), jnp.float32)]
    if prefix:
        shapes.append(jax.ShapeDtypeStruct((tokens.shape[0], PREFIX), tokens.dtype))
    found = pl.pallas_call(
        kernel,
        out_shape=shapes,
        in_specs=[ANY] * len(after) + [VMEM] * (2 + len(partial)),
        out_specs=[VMEM] * len(shapes),
        scratch_shapes=[pltpu.VMEM((count, places * qtok), jnp.float32)],
        compiler_params=params(),
        cost_estimate=pl.CostEstimate(
            flops=4 * tokens.shape[0] * places * qtok * 128, bytes_accessed=4 << 20, transcendentals=0
        ),
    )(*after, tokens, queries, *partial)
    return found if prefix else found[0]


def pick_kernel(count, order, coarse_ref, ids_ref, returned_ref, exact_out, coarse_out, picked_ref, sems):
    coarse_copy = pltpu.make_async_copy(coarse_ref, coarse_out, sems.at[0])
    exact_copy = pltpu.make_async_copy(picked_ref, exact_out, sems.at[1])
    coarse_copy.start()
    ids = ids_ref[...]
    short = ids.shape[1]
    source = (ids // count) ^ lax.axis_index("slab")
    block, scale = jnp.zeros_like(ids), 1
    for low, size in reversed(order):
        block = block + ((source // low) % size) * scale
        scale *= size
    place = block * count + ids % count
    lanes = 128
    rows = returned_ref.shape[1] // lanes
    table = jnp.concatenate([returned_ref[:, r * lanes : (r + 1) * lanes] for r in range(rows)], axis=0)
    hot = lax.broadcasted_iota(jnp.int32, (lanes, short), 0) == place % lanes
    hot = jnp.where(hot, 1.0, 0.0).astype(jnp.bfloat16)
    column = None
    rest = table
    for _ in range(3):
        term = rest.astype(jnp.bfloat16)
        rest = rest - term.astype(jnp.float32)
        part = lax.dot_general(term, hot, (((1,), (0,)), ((), ())), preferred_element_type=jnp.float32)
        column = part if column is None else column + part
    mine = lax.broadcasted_iota(jnp.int32, (rows, short), 0) == place // lanes
    picked_ref[...] = jnp.sum(jnp.where(mine, column, 0.0), axis=0, keepdims=True)
    exact_copy.start()
    coarse_copy.wait()
    exact_copy.wait()


def exchange(array, offset, owners):
    return lax.ppermute(array, "slab", [(i, i ^ offset) for i in range(owners)])


def join(*parts):
    return jnp.concatenate(parts, axis=0)


def stages(owners):
    found, low = [], 1
    while low < owners:
        size = min(4, owners // low)
        found.append((low, size))
        low *= size
    return found[::-1]


def per_device(queries, passages, lengths, shortlist):
    owners = lax.axis_size("slab")
    count = passages.shape[0]
    order = stages(owners)
    half = owners // 2
    held = queries
    full = None
    for low, size in order:
        came = [exchange(held, low * k, owners) for k in range(1, size)]
        parts = [held] + came
        if held is queries:
            full = live_tokens(lengths, passages)
            parts[-2], parts[-1], full = lax.optimization_barrier((parts[-2], parts[-1], full))
        if len(parts) * held.shape[0] < owners:
            held = join(*parts)
    scores = [score(exact_kernel, half, count, full, join(*parts[: size // 2]))]
    for part in parts[size // 2 :]:
        scores.append(score(exact_kernel, part.shape[0], count, full, part))
    result = None
    rows = join(*scores)
    for low, size in reversed(order):
        group = rows.shape[0] // size
        away = [exchange(rows[group * k : group * (k + 1)], low * k, owners) for k in reversed(range(1, size))]
        rows = jnp.concatenate([rows[:group]] + away[::-1], axis=1)
        if result is None:
            near_kernel = functools.partial(near_coarse_kernel, order, held.shape[0])
            far_kernel = functools.partial(far_coarse_kernel, order, held.shape[0], owners - held.shape[0])
            result, prefix = score(near_kernel, owners, count, full, held, after=scores, prefix=True)
            result = score(far_kernel, owners, count, prefix, join(*came), partial=(result,))
    exact, result = pl.pallas_call(
        functools.partial(pick_kernel, count, order),
        out_shape=(
            jax.ShapeDtypeStruct(shortlist.shape, jnp.float32),
            jax.ShapeDtypeStruct(result.shape, jnp.float32),
        ),
        in_specs=[VMEM, VMEM, VMEM],
        out_specs=(ANY, ANY),
        scratch_shapes=[pltpu.VMEM(shortlist.shape, jnp.float32), pltpu.SemaphoreType.DMA((2,))],
        compiler_params=params(),
    )(result, shortlist, rows)
    return (result.T, exact)


def solution(mesh):
    return jax.shard_map(
        per_device,
        mesh=mesh,
        in_specs=(
            P(("groups", "slab"), None, None),
            P(("groups", "slab"), None, None),
            P(("groups", "slab")),
            P(("groups", "slab"), None),
        ),
        out_specs=(P(("groups", "slab"), None), P(("groups", "slab"), None)),
        check_vma=False,
    )
```
